32 devices in a mesh: req: 16 (over z, y, x), tp: 2 (over core).
Axes of the slice: x: 2, y: 2, z: 4, core: 2. Of those that a mesh axis runs over, the one named last changes fastest.
Arguments:
- q_proj: bfloat16 [16, 128, 768], P('req', None, 'tp'), may hold values from -24 to 24, as said below
- kv_proj: bfloat16 [16, 128, 2, 256], P('req', None, None, 'tp'), may hold values from -6 to 6
- q_bias: bfloat16 [768], P('tp'), may hold values from -3 to 3
- kv_bias: bfloat16 [2, 256], P(None, 'tp'), may hold values from -3 to 3
- prefix_kv: bfloat16 [16, 1024, 2, 256], P('req', None, None, 'tp'), may hold values from -24 to 24, as said below
- lengths: int32 [16], P('req'), may hold values from 1 to 128, 1024 in all
- group_of: int32 [16], P('req'), may hold values from 0 to 2
- owner: int32 [3], replicated, may hold values from 0 to 15
- positions: int32 [16, 128], P('req'), may hold values from 1024 to 1278, as said below
- residual: bfloat16 [16, 128, 5120], P('req', None, 'tp'), may hold values from -6 to 6
- out_weight: bfloat16 [768, 5120], P(None, 'tp'), may hold values from -0.21875 to 0.21875
Outputs:
- hidden: bfloat16 [16, 128, 5120], P('req', None, 'tp')
The draws below stay inside these ranges and needn't reach their ends.
Inputs may be any that keep to these rules, and one draw needn't show every extreme that they name: `q_proj`: projected queries; entries stay within the stated bounds. `prefix_kv`: cached keys are already rotated at prefix positions 0 to 1023. Each request's positions are a start of 1024 or more plus the slot index.
All inputs are finite; a program needn't handle non-finite values. No bound on the sum of `lengths` on one device may be relied on, other than what follows from the above.
Results may differ from the reference program's by a relative error of at most 0.006.
Values may be sent and summed in bfloat16 or wider, within the bound.
A program may use at most 128 MiB of HBM per device.

```python
import math
import jax
import jax.numpy as jnp
import numpy as np
from jax import lax

D = 5120
HD = 128
HQ_DEV = 3
GROUPS = 3
CAP = 128
PREFIX = 1024
KVH = 2
HEADS = 6
N_REQ = 16


def draw_q_proj(key, part):
    base = jnp.clip(jax.random.normal(jax.random.fold_in(key, 1), (N_REQ, CAP, HEADS * HD), jnp.float32), -6.0, 6.0)
    return base.astype(jnp.bfloat16)


def draw_prefix_kv(key, part):
    base = jnp.clip(jax.random.normal(jax.random.fold_in(key, 3), (N_REQ, PREFIX, 2, KVH * HD), jnp.float32), -6.0, 6.0)
    return base.astype(jnp.bfloat16)


def draw_positions(key, part):
    start = jax.random.randint(jax.random.fold_in(key, 5), (N_REQ, 1), PREFIX, PREFIX + CAP)
    start = start.at[0, 0].set(PREFIX + CAP - 1)
    start = start.at[1, 0].set(PREFIX)
    return (start + jnp.arange(CAP)[None, :]).astype(jnp.int32)


def with_ends(values, rng, least, largest):
    place = [jax.random.randint(jax.random.fold_in(rng, axis), (), 0, length) for axis, length in enumerate(values.shape)]
    main_axis = values.shape.index(max(values.shape))
    neighbour = place[:main_axis] + [(place[main_axis] + 1) % values.shape[main_axis]] + place[main_axis + 1:]
    return values.at[tuple(place)].set(least).at[tuple(neighbour)].set(largest)


def level_of(own_key, shape, shards, smallest, top_value):
    def one(position, blocks):
        draws = jax.random.uniform(jax.random.fold_in(jax.random.fold_in(own_key, 6), position), (blocks,), jnp.float32, smallest / len(shards), top_value / len(shards))
        return jnp.repeat(jnp.exp(draws), shape[position] // blocks).reshape((-1,) + (1,) * (len(shape) - position - 1))

    factor_of = one(*shards[0])
    for cut in shards[1:]:
        factor_of = factor_of * one(*cut)
    return factor_of


def length_profile(count, total, most, lean):
    loads = [(1 << 20) // math.isqrt(standing ** lean) + 1 for standing in range(2, count + 1)]
    rest, holding = total - most - (count - 1), [1] * (count - 1)
    while rest > 0:
        candidates = [i for i in range(count - 1) if holding[i] < most]
        whole, budget = sum([loads[i] for i in candidates]), rest
        for i in candidates:
            addition = min(most - holding[i], max(1, budget * loads[i] // whole), rest)
            holding[i] = holding[i] + addition
            rest = rest - addition
    return np.array([most] + holding)


def uneven_parts(key, number_of, total, limit, skew):
    if number_of == 2:
        one = jax.random.randint(key, (), max(1, total - limit), min(limit, total - 1) + 1)
        return jnp.stack([one, total - one])
    sizes = jnp.asarray(length_profile(number_of, total, limit, skew), jnp.int32)
    couples = (number_of - 1) // 2
    source_of, sink = sizes[1:1 + 2 * couples:2], sizes[2:2 + 2 * couples:2]
    room = jnp.minimum(source_of - 1, limit - sink)
    moved = jax.random.randint(jax.random.fold_in(key, 1), (couples,), 0, 1 << 20) % (room + 1)
    sizes = sizes.at[1:1 + 2 * couples:2].set(source_of - moved).at[2:2 + 2 * couples:2].set(sink + moved)
    return sizes[jax.random.permutation(jax.random.fold_in(key, 2), number_of)]


def normal_values(own_key, extent, width, bound, split=(), kind=jnp.bfloat16):
    gain = level_of(own_key, extent, split, -0.22, 0.18) if split else 1.0
    entries = jax.random.normal(own_key, extent, jnp.float32) * width * gain
    return jnp.minimum(jnp.maximum(entries, -bound), bound).astype(kind)


def setup_inputs(seed: int = 0) -> dict:
    arg_keys = jax.random.split(jax.random.key(seed), 12)
    q_proj = draw_q_proj(jax.random.fold_in(arg_keys[11], 71), 0)
    kv_proj = normal_values(arg_keys[1], (N_REQ, CAP, 2, KVH * HD), 1.0, 6.0, ((0, 16), (3, 2)))
    q_bias = normal_values(arg_keys[2], (HEADS * HD,), 0.5, 3.0, ((0, 2),))
    kv_bias = normal_values(arg_keys[3], (2, KVH * HD), 0.5, 3.0, ((1, 2),))
    prefix_kv = draw_prefix_kv(jax.random.fold_in(arg_keys[11], 71), 0)
    lengths = uneven_parts(arg_keys[5], N_REQ, N_REQ * CAP // 2, CAP, 2).astype(jnp.int32)
    group_of = with_ends(jax.random.randint(arg_keys[6], (N_REQ,), 0, GROUPS), jax.random.fold_in(arg_keys[6], 1), 0, GROUPS - 1).astype(jnp.int32)
    owner = jax.random.randint(arg_keys[7], (GROUPS,), 0, N_REQ).astype(jnp.int32)
    positions = draw_positions(jax.random.fold_in(arg_keys[11], 71), 0)
    residual = normal_values(arg_keys[9], (N_REQ, CAP, D), 1.0, 6.0, ((0, 16), (2, 2)))
    out_weight = normal_values(arg_keys[10], (HEADS * HD, D), (HEADS * HD) ** -0.5, 0.21875, ((1, 2),))
    return {"q_proj": q_proj, "kv_proj": kv_proj, "q_bias": q_bias, "kv_bias": kv_bias, "prefix_kv": prefix_kv, "lengths": lengths, "group_of": group_of, "owner": owner, "positions": positions, "residual": residual, "out_weight": out_weight}


def rotate(vectors, places):
    half = HD // 2
    index = jnp.arange(half).astype(jnp.float32)
    freqs = jnp.exp(index * (-2.0 / HD) * math.log(1000000.0))
    angles = places.astype(jnp.float32)[:, None] * freqs[None, :]
    cosine = jnp.concatenate([jnp.cos(angles), jnp.cos(angles)], axis=-1)[:, None, :]
    sine = jnp.concatenate([jnp.sin(angles), jnp.sin(angles)], axis=-1)[:, None, :]
    turned = jnp.concatenate([-vectors[..., half:], vectors[..., :half]], axis=-1)
    return vectors * cosine + turned * sine

def attend(queries, keys, vals, allowed):
    scores = jnp.einsum('rhd,kd->hrk', queries.astype(jnp.float32), keys.astype(jnp.float32)) * (1.0 / math.sqrt(HD))
    scores = jnp.where(allowed[None], scores, -1e+30)
    top = lax.optimization_barrier(jnp.max(scores, axis=-1, keepdims=True))
    weights = jnp.where(allowed[None], jnp.exp(scores - top), 0.0)
    total = lax.optimization_barrier(jnp.sum(weights, axis=-1))
    rounded = weights.astype(jnp.bfloat16)
    mixed = jnp.einsum('hrk,kd->rhd', rounded.astype(jnp.float32), vals.astype(jnp.float32))
    return mixed / jnp.transpose(total)[:, :, None]

def reference(q_proj, kv_proj, q_bias, kv_bias, prefix_kv, lengths, group_of, owner, positions, residual, out_weight):

    def one_request(items):
        q_rows, kv_rows, length, group, places, resid = items
        owner_col = owner[group].astype(jnp.int32)
        slab = lax.dynamic_index_in_dim(prefix_kv, owner_col, 0, keepdims=False).reshape(PREFIX, 2, KVH, HD)
        queries = q_rows.astype(jnp.float32).reshape(CAP, HEADS, HD) + q_bias.astype(jnp.float32).reshape(HEADS, HD)
        queries = rotate(queries, places).astype(jnp.bfloat16)
        pairs = kv_rows.astype(jnp.float32).reshape(CAP, 2, KVH, HD) + kv_bias.astype(jnp.float32).reshape(2, KVH, HD)
        keys = rotate(pairs[:, 0], places).astype(jnp.bfloat16)
        vals = pairs[:, 1].astype(jnp.bfloat16)
        all_keys = jnp.concatenate([slab[:, 0], keys], axis=0)
        all_vals = jnp.concatenate([slab[:, 1], vals], axis=0)
        slots = jnp.arange(CAP).astype(jnp.int32)
        causal = slots[None, :] <= slots[:, None]
        allowed = jnp.concatenate([jnp.ones((CAP, PREFIX), dtype=bool), causal], axis=1)
        heads = []
        for kv_head in range(KVH):
            heads.append(attend(queries[:, kv_head * HQ_DEV:(kv_head + 1) * HQ_DEV], all_keys[:, kv_head], all_vals[:, kv_head], allowed))
        mixed = jnp.concatenate(heads, axis=1)
        mixed = jnp.where((slots < length)[:, None, None], mixed, 0.0).astype(jnp.bfloat16).reshape(CAP, HEADS * HD)
        proj = jnp.dot(mixed, out_weight, preferred_element_type=jnp.float32)
        return (resid.astype(jnp.float32) + proj).astype(jnp.bfloat16)
    return lax.map(one_request, (q_proj, kv_proj, lengths, group_of, positions, residual))
```

```python
import functools
import math

import jax
import jax.numpy as jnp
from jax import lax
from jax.experimental import pallas as pl
from jax.experimental.pallas import tpu as pltpu
from jax.sharding import PartitionSpec as P

HD = 128
QUAD = 4
PIECES = 4
MESH = pl.DeviceIdType.MESH
BF16 = jnp.bfloat16
F32 = jnp.float32


def kernel(
    n_req,
    n_tp,
    groups,
    length_ref,
    group_ref,
    owner_ref,
    pos_ref,
    q_hbm,
    kv_hbm,
    qb_hbm,
    kvb_hbm,
    slab_hbm,
    res_hbm,
    w_hbm,
    out_ref,
    q_in,
    kv_in,
    qb_in,
    kvb_in,
    res_in,
    w_in,
    queries,
    split,
    gsend,
    grecv,
    gsmem,
    att_all,
    total_ref,
    p1,
    chain,
    fwd,
    outp,
    kvp,
    local_sem,
    p1_send,
    p1_recv,
    ch_send,
    ch_recv,
    p3_send,
    p3_recv,
    g_send,
    g_recv,
    att_send,
    att_recv,
):
    req = lax.axis_index("req")
    tp = lax.axis_index("tp")
    depth = n_req // QUAD
    k = req // QUAD
    q = req % QUAD
    base = k * QUAD
    rows = p1[0].shape[1]
    cap = q_in.shape[0]
    heads = q_in.shape[1] // HD
    feats = q_in.shape[1]

    def mate(d):
        return base + (q + d) % QUAD

    fetches = []
    for i, (src, dst) in enumerate(
        ((q_hbm, q_in), (kv_hbm, kv_in), (qb_hbm, qb_in), (kvb_hbm, kvb_in), (res_hbm, res_in), (w_hbm, w_in))
    ):
        fetches.append(pltpu.make_async_copy(src, dst, local_sem.at[i]))
    for f in fetches[:4]:
        f.start()

    barrier = pltpu.get_barrier_semaphore()
    for d in range(1, QUAD):
        pl.semaphore_signal(barrier, inc=1, device_id=(mate(d), tp), device_id_type=MESH)
    for d in range(1, n_tp):
        pl.semaphore_signal(barrier, inc=1, device_id=(req, (tp + d) % n_tp), device_id_type=MESH)

    @pl.when(k > 0)
    def _():
        pl.semaphore_signal(barrier, inc=1, device_id=(req - QUAD, tp), device_id_type=MESH)

    @pl.when(k < depth - 1)
    def _():
        pl.semaphore_signal(barrier, inc=1, device_id=(req + QUAD, tp), device_id_type=MESH)

    gsend[...] = jnp.full(gsend.shape, group_ref[0], jnp.int32)
    ends = jnp.where(k > 0, 1, 0) + jnp.where(k < depth - 1, 1, 0)
    pl.semaphore_wait(barrier, QUAD - 1 + n_tp - 1 + ends)

    gcopies = []
    for d in range(1, QUAD):
        c = pltpu.make_async_remote_copy(
            src_ref=gsend,
            dst_ref=grecv.at[d - 1],
            send_sem=g_send.at[d - 1],
            recv_sem=g_recv.at[d - 1],
            device_id=(mate(d), tp),
            device_id_type=MESH,
        )
        gcopies.append(c)

    first, own = [], []
    for m in range(PIECES):
        line = []
        for d in range(1, QUAD):
            to = (q + d) % QUAD
            start = pl.multiple_of((to * PIECES + m) * rows, rows)
            c = pltpu.make_async_remote_copy(
                src_ref=slab_hbm.at[pl.ds(start, rows)],
                dst_ref=p1[m].at[q],
                send_sem=p1_send.at[m, d - 1],
                recv_sem=p1_recv.at[m, d - 1],
                device_id=(mate(d), tp),
                device_id_type=MESH,
            )
            c.start()
            line.append(c)
        start = pl.multiple_of((q * PIECES + m) * rows, rows)
        c = pltpu.make_async_copy(slab_hbm.at[pl.ds(start, rows)], p1[m].at[q], local_sem.at[6 + m])
        c.start()
        own.append(c)
        first.append(line)
        if m == 0:
            for g in gcopies:
                g.start()
    for f in fetches[4:]:
        f.start()

    for f in fetches[:4]:
        f.wait()
    lane = lax.broadcasted_iota(jnp.int32, (cap, HD), 1)
    place = (pos_ref[0, 0] + lax.broadcasted_iota(jnp.int32, (cap, HD), 0)).astype(F32)
    index = (lane % (HD // 2)).astype(F32)
    freqs = jnp.exp(index * (-2.0 / HD) * math.log(1000000.0))
    angles = place * freqs
    cosine = jnp.cos(angles)
    sine = jnp.sin(angles)
    sine = jnp.where(lane < HD // 2, -sine, sine)

    def rot(x):
        return x * cosine + pltpu.roll(x, HD // 2, 1) * sine

    for h in range(heads):
        cols = pl.ds(h * HD, HD)
        x = q_in[:, cols].astype(F32) + qb_in[:, cols].astype(F32)
        queries[pl.ds(h * cap, cap), :] = rot(x).astype(BF16)
    split[pl.ds(0, 2 * cap), :] = kv_in[...].astype(F32)
    bias = kvb_in[...].astype(F32)
    keys = rot(split[pl.ds(0, cap, stride=2), :] + bias[0:1, :]).astype(BF16)
    vals = (split[pl.ds(1, cap, stride=2), :] + bias[1:2, :]).astype(BF16)
    scale = 1.0 / math.sqrt(HD)
    nt = (((1,), (1,)), ((), ()))

    qs = queries[...]
    s = lax.dot_general(qs, keys, nt, preferred_element_type=F32) * scale
    seen = lax.broadcasted_iota(jnp.int32, s.shape, 1) <= lax.broadcasted_iota(jnp.int32, s.shape, 0) % cap
    s = jnp.where(seen, s, -1e30)
    top = jnp.max(s, axis=-1, keepdims=True)
    w = jnp.where(seen, jnp.exp(s - top), 0.0)
    tot = jnp.sum(w, axis=-1, keepdims=True)
    acc = jnp.dot(w.astype(BF16), vals, preferred_element_type=F32)

    for d in range(1, QUAD):
        gcopies[d - 1].wait_recv()
    to_smem = pltpu.make_async_copy(grecv, gsmem, local_sem.at[6 + PIECES])
    to_smem.start()
    to_smem.wait()
    wants = [group_ref[0]]
    for d in range(1, QUAD):
        wants.append(gsmem[QUAD - d - 1, 0, 0])

    near = jnp.where(k < depth // 2, 0, 1)

    def chain_copy(m, d):
        step = 1 - 2 * d
        return pltpu.make_async_remote_copy(
            src_ref=fwd[m].at[d],
            dst_ref=chain[m].at[d],
            send_sem=ch_send.at[m, d],
            recv_sem=ch_recv.at[m, d],
            device_id=(req + step * QUAD, tp),
            device_id_type=MESH,
        )

    def has_source(d):
        return jnp.where(d == 0, k, depth - 1 - k) > 0

    def has_target(d):
        return jnp.where(d == 0, depth - 1 - k, k) > 0

    last = []

    def stage_two(m):
        for c in first[m]:
            c.wait_recv()
        own[m].wait()
        for d in (near, 1 - near):

            @pl.when(has_source(d))
            def _():
                chain_copy(m, d).wait_recv()

            @pl.when(has_target(d))
            def _():
                for c in range(groups):
                    o = owner_ref[c]
                    mine = p1[m][o % QUAD]
                    fwd[m][d, c] = jnp.where(o // QUAD == k, mine, chain[m][d, c])
                chain_copy(m, d).start()

        line = []
        for d in (1, 2, 3, 0):
            c = wants[d]
            o = owner_ref[c]
            oz = o // QUAD
            other = jnp.where(oz < k, chain[m][0, c], chain[m][1, c])
            piece = jnp.where(oz == k, p1[m][o % QUAD], other)
            if d == 0:
                kvp[m][q] = piece
            else:
                outp[m][d - 1] = piece
                r = pltpu.make_async_remote_copy(
                    src_ref=outp[m].at[d - 1],
                    dst_ref=kvp[m].at[q],
                    send_sem=p3_send.at[m, d - 1],
                    recv_sem=p3_recv.at[m, d - 1],
                    device_id=(mate(d), tp),
                    device_id_type=MESH,
                )
                r.start()
                line.append(r)
        last.append(line)

    def attend(m, top, tot, acc):
        for r in last[m]:
            r.wait_recv()
        for j in range(QUAD):
            split[pl.ds(j * rows, rows), :] = kvp[m][j].astype(F32)
        half = QUAD * rows // 2
        ks = split[pl.ds(0, half, stride=2), :].astype(BF16)
        vs = split[pl.ds(1, half, stride=2), :].astype(BF16)
        s = lax.dot_general(queries[...], ks, nt, preferred_element_type=F32) * scale
        new = jnp.maximum(top, jnp.max(s, axis=-1, keepdims=True))
        fade = jnp.exp(top - new)
        w = jnp.exp(s - new)
        tot = tot * fade + jnp.sum(w, axis=-1, keepdims=True)
        acc = acc * fade + jnp.dot(w.astype(BF16), vs, preferred_element_type=F32)
        return new, tot, acc

    for m in range(PIECES):
        stage_two(m)
        if m > 0:
            top, tot, acc = attend(m - 1, top, tot, acc)
    top, tot, acc = attend(PIECES - 1, top, tot, acc)

    mixed = acc / tot
    slot = lax.broadcasted_iota(jnp.int32, mixed.shape, 0) % cap
    mixed = jnp.where(slot < length_ref[0], mixed, 0.0).astype(BF16)
    for h in range(heads):
        att_all[tp, :, pl.ds(h * HD, HD)] = mixed[h * cap : (h + 1) * cap, :]
    attc = []
    for d in range(1, n_tp):
        c = pltpu.make_async_remote_copy(
            src_ref=att_all.at[tp],
            dst_ref=att_all.at[tp],
            send_sem=att_send.at[d - 1],
            recv_sem=att_recv.at[d - 1],
            device_id=(req, (tp + d) % n_tp),
            device_id_type=MESH,
        )
        c.start()
        attc.append(c)
    for f in fetches[4:]:
        f.wait()
    width = out_ref.shape[1]
    tile = 640 if width % 640 == 0 else width
    for d in range(n_tp):
        t = (tp + n_tp - d) % n_tp
        if d > 0:
            attc[d - 1].wait_recv()
        a = att_all[t]
        wrows = pl.ds(pl.multiple_of(t * feats, feats), feats)
        for n in range(width // tile):
            cols = pl.ds(n * tile, tile)
            part = jnp.dot(a, w_in[wrows, cols], preferred_element_type=F32)
            if d == 0:
                part = part + res_in[:, cols].astype(F32)
            else:
                part = part + total_ref[:, cols]
            if d < n_tp - 1:
                total_ref[:, cols] = part
            else:
                out_ref[:, cols] = part.astype(out_ref.dtype)

    for g in gcopies:
        g.wait_send()
    for line in first + last:
        for c in line:
            c.wait_send()
    for m in range(PIECES):
        for d in (0, 1):

            @pl.when(has_target(d))
            def _():
                chain_copy(m, d).wait_send()

    for c in attc:
        c.wait_send()


def body(
    n_req,
    n_tp,
    q_proj,
    kv_proj,
    q_bias,
    kv_bias,
    prefix_kv,
    lengths,
    group_of,
    owner,
    positions,
    residual,
    out_weight,
):
    cap, feats = q_proj.shape[1:]
    total = prefix_kv.shape[1] * 2
    rows = total // (QUAD * PIECES)
    groups = owner.shape[0]
    width = residual.shape[2]
    smem = pl.BlockSpec(memory_space=pltpu.SMEM)
    anym = pl.BlockSpec(memory_space=pl.ANY)
    dma = pltpu.SemaphoreType.DMA

    out = pl.pallas_call(
        functools.partial(kernel, n_req, n_tp, groups),
        out_shape=jax.ShapeDtypeStruct((cap, width), BF16),
        in_specs=[smem] * 4 + [anym] * 7,
        out_specs=pl.BlockSpec(memory_space=pltpu.VMEM),
        scratch_shapes=[
            pltpu.VMEM((cap, feats), BF16),
            pltpu.VMEM((2 * cap, HD), BF16),
            pltpu.VMEM((1, feats), BF16),
            pltpu.VMEM((2, HD), BF16),
            pltpu.VMEM((cap, width), BF16),
            pltpu.VMEM(out_weight.shape, BF16),
            pltpu.VMEM((feats, HD), BF16),
            pltpu.VMEM((max(2 * cap, QUAD * rows), HD), F32),
            pltpu.VMEM((8, 128), jnp.int32),
            pltpu.VMEM((QUAD - 1, 8, 128), jnp.int32),
            pltpu.SMEM((QUAD - 1, 8, 128), jnp.int32),
            pltpu.VMEM((n_tp, cap, feats), BF16),
            pltpu.VMEM((cap, width), F32),
            [pltpu.VMEM((QUAD, rows, HD), BF16)] * PIECES,
            [pltpu.VMEM((2, groups, rows, HD), BF16)] * PIECES,
            [pltpu.VMEM((2, groups, rows, HD), BF16)] * PIECES,
            [pltpu.VMEM((QUAD - 1, rows, HD), BF16)] * PIECES,
            [pltpu.VMEM((QUAD, rows, HD), BF16)] * PIECES,
            dma((7 + PIECES,)),
            dma((PIECES, QUAD - 1)),
            dma((PIECES, QUAD - 1)),
            dma((PIECES, 2)),
            dma((PIECES, 2)),
            dma((PIECES, QUAD - 1)),
            dma((PIECES, QUAD - 1)),
            dma((QUAD - 1,)),
            dma((QUAD - 1,)),
            dma((max(n_tp - 1, 1),)),
            dma((max(n_tp - 1, 1),)),
        ],
        compiler_params=pltpu.CompilerParams(
            collective_id=0, has_side_effects=True, vmem_limit_bytes=60 * 1024 * 1024
        ),
        cost_estimate=pl.CostEstimate(
            flops=2 * cap * out_weight.shape[0] * width + 4 * cap * feats * (total // 2 + cap),
            bytes_accessed=2 * (out_weight.size + 2 * cap * width + total * HD),
            transcendentals=cap * feats // HD * (total // 2 + cap),
        ),
    )(
        lengths,
        group_of,
        owner,
        positions,
        q_proj[0],
        kv_proj[0].reshape(2 * cap, HD),
        q_bias.reshape(1, feats),
        kv_bias,
        prefix_kv[0].reshape(total, HD),
        residual[0],
        out_weight,
    )
    return out[None]


def solution(mesh):
    in_specs = (
        P("req", None, "tp"),
        P("req", None, None, "tp"),
        P("tp"),
        P(None, "tp"),
        P("req", None, None, "tp"),
        P("req"),
        P("req"),
        P(),
        P("req", None),
        P("req", None, "tp"),
        P(None, "tp"),
    )
    out_specs = P("req", None, "tp")
    run = functools.partial(body, mesh.shape["req"], mesh.shape["tp"])
    return jax.shard_map(run, mesh=mesh, in_specs=in_specs, out_specs=out_specs, check_vma=False)
```

```python
import functools
import math

import jax
import jax.numpy as jnp
from jax import lax
from jax.experimental import pallas as pl
from jax.experimental.pallas import tpu as pltpu
from jax.sharding import PartitionSpec as P

HD = 128
QUAD = 4
PIECES = 4
MESH = pl.DeviceIdType.MESH
BF16 = jnp.bfloat16
F32 = jnp.float32


def kernel(
    n_req,
    n_tp,
    groups,
    length_ref,
    group_ref,
    owner_ref,
    pos_ref,
    q_hbm,
    kv_hbm,
    qb_hbm,
    kvb_hbm,
    slab_hbm,
    res_hbm,
    w_hbm,
    out_ref,
    q_in,
    kv_in,
    qb_in,
    kvb_in,
    res_in,
    w_in,
    queries,
    split,
    gsend,
    grecv,
    gsmem,
    att_all,
    total_ref,
    p1,
    chain,
    fwd,
    outp,
    kvp,
    local_sem,
    p1_send,
    p1_recv,
    ch_send,
    ch_recv,
    p3_send,
    p3_recv,
    g_send,
    g_recv,
    att_send,
    att_recv,
):
    req = lax.axis_index("req")
    tp = lax.axis_index("tp")
    depth = n_req // QUAD
    k = req // QUAD
    q = req % QUAD
    base = k * QUAD
    rows = p1[0].shape[1]
    cap = q_in.shape[0]
    heads = q_in.shape[1] // HD
    feats = q_in.shape[1]

    def mate(d):
        return base + (q + d) % QUAD

    fetches = []
    for i, (src, dst) in enumerate(
        ((q_hbm, q_in), (kv_hbm, kv_in), (qb_hbm, qb_in), (kvb_hbm, kvb_in), (res_hbm, res_in), (w_hbm, w_in))
    ):
        fetches.append(pltpu.make_async_copy(src, dst, local_sem.at[i]))
    for f in fetches[:4]:
        f.start()

    barrier = pltpu.get_barrier_semaphore()
    for d in range(1, QUAD):
        pl.semaphore_signal(barrier, inc=1, device_id=(mate(d), tp), device_id_type=MESH)
    for d in range(1, n_tp):
        pl.semaphore_signal(barrier, inc=1, device_id=(req, (tp + d) % n_tp), device_id_type=MESH)

    @pl.when(k > 0)
    def _():
        pl.semaphore_signal(barrier, inc=1, device_id=(req - QUAD, tp), device_id_type=MESH)

    @pl.when(k < depth - 1)
    def _():
        pl.semaphore_signal(barrier, inc=1, device_id=(req + QUAD, tp), device_id_type=MESH)

    gsend[...] = jnp.full(gsend.shape, group_ref[0], jnp.int32)
    ends = jnp.where(k > 0, 1, 0) + jnp.where(k < depth - 1, 1, 0)
    pl.semaphore_wait(barrier, QUAD - 1 + n_tp - 1 + ends)

    gcopies = []
    for d in range(1, QUAD):
        c = pltpu.make_async_remote_copy(
            src_ref=gsend,
            dst_ref=grecv.at[d - 1],
            send_sem=g_send.at[d - 1],
            recv_sem=g_recv.at[d - 1],
            device_id=(mate(d), tp),
            device_id_type=MESH,
        )
        gcopies.append(c)

    first, own = [], []
    for m in range(PIECES):
        line = []
        for d in range(1, QUAD):
            to = (q + d) % QUAD
            start = pl.multiple_of((to * PIECES + m) * rows, rows)
            c = pltpu.make_async_remote_copy(
                src_ref=slab_hbm.at[pl.ds(start, rows)],
                dst_ref=p1[m].at[q],
                send_sem=p1_send.at[m, d - 1],
                recv_sem=p1_recv.at[m, d - 1],
                device_id=(mate(d), tp),
                device_id_type=MESH,
            )
            c.start()
            line.append(c)
        start = pl.multiple_of((q * PIECES + m) * rows, rows)
        c = pltpu.make_async_copy(slab_hbm.at[pl.ds(start, rows)], p1[m].at[q], local_sem.at[6 + m])
        c.start()
        own.append(c)
        first.append(line)
        if m == 0:
            for g in gcopies:
                g.start()
    for f in fetches[4:]:
        f.start()

    for f in fetches[:4]:
        f.wait()
    lane = lax.broadcasted_iota(jnp.int32, (cap, HD), 1)
    place = (pos_ref[0, 0] + lax.broadcasted_iota(jnp.int32, (cap, HD), 0)).astype(F32)
    index = (lane % (HD // 2)).astype(F32)
    freqs = jnp.exp(index * (-2.0 / HD) * math.log(1000000.0))
    angles = place * freqs
    cosine = jnp.cos(angles)
    sine = jnp.sin(angles)
    sine = jnp.where(lane < HD // 2, -sine, sine)

    def rot(x):
        return x * cosine + pltpu.roll(x, HD // 2, 1) * sine

    for h in range(heads):
        cols = pl.ds(h * HD, HD)
        x = q_in[:, cols].astype(F32) + qb_in[cols].astype(F32)[None, :]
        queries[pl.ds(h * cap, cap), :] = rot(x).astype(BF16)
    split[pl.ds(0, 2 * cap), :] = kv_in[...].astype(F32)
    bias = kvb_in[...].astype(F32)
    keys = rot(split[pl.ds(0, cap, stride=2), :] + bias[0:1, :]).astype(BF16)
    vals = (split[pl.ds(1, cap, stride=2), :] + bias[1:2, :]).astype(BF16)
    scale = 1.0 / math.sqrt(HD)
    nt = (((1,), (1,)), ((), ()))

    qs = queries[...]
    s = lax.dot_general(qs, keys, nt, preferred_element_type=F32) * scale
    seen = lax.broadcasted_iota(jnp.int32, s.shape, 1) <= lax.broadcasted_iota(jnp.int32, s.shape, 0) % cap
    s = jnp.where(seen, s, -1e30)
    top = jnp.max(s, axis=-1, keepdims=True)
    w = jnp.where(seen, jnp.exp(s - top), 0.0)
    tot = jnp.sum(w, axis=-1, keepdims=True)
    acc = jnp.dot(w.astype(BF16), vals, preferred_element_type=F32)

    for d in range(1, QUAD):
        gcopies[d - 1].wait_recv()
    to_smem = pltpu.make_async_copy(grecv, gsmem, local_sem.at[6 + PIECES])
    to_smem.start()
    to_smem.wait()
    wants = [group_ref[0]]
    for d in range(1, QUAD):
        wants.append(gsmem[QUAD - d - 1, 0, 0])

    near = jnp.where(k < depth // 2, 0, 1)

    def chain_copy(m, d):
        step = 1 - 2 * d
        return pltpu.make_async_remote_copy(
            src_ref=fwd[m].at[d],
            dst_ref=chain[m].at[d],
            send_sem=ch_send.at[m, d],
            recv_sem=ch_recv.at[m, d],
            device_id=(req + step * QUAD, tp),
            device_id_type=MESH,
        )

    def has_target(d):
        return jnp.where(d == 0, depth - 1 - k, k) > 0

    is_end = jnp.logical_or(k == 0, k == depth - 1)
    last = []

    def arrive(m):
        for c in first[m]:
            c.wait_recv()
        own[m].wait()

    def forward(m, d):
        for c in range(groups):
            o = owner_ref[c]
            mine = p1[m][o % QUAD]
            fwd[m][d, c] = jnp.where(o // QUAD == k, mine, chain[m][d, c])
        chain_copy(m, d).start()

    def hand_out(m):
        line = []
        for d in (1, 2, 3, 0):
            c = wants[d]
            o = owner_ref[c]
            oz = o // QUAD
            other = jnp.where(oz < k, chain[m][0, c], chain[m][1, c])
            piece = jnp.where(oz == k, p1[m][o % QUAD], other)
            if d == 0:
                kvp[m][q] = piece
            else:
                outp[m][d - 1] = piece
                r = pltpu.make_async_remote_copy(
                    src_ref=outp[m].at[d - 1],
                    dst_ref=kvp[m].at[q],
                    send_sem=p3_send.at[m, d - 1],
                    recv_sem=p3_recv.at[m, d - 1],
                    device_id=(mate(d), tp),
                    device_id_type=MESH,
                )
                r.start()
                line.append(r)
        last.append(line)

    def attend(m, top, tot, acc):
        for r in last[m]:
            r.wait_recv()
        for j in range(QUAD):
            split[pl.ds(j * rows, rows), :] = kvp[m][j].astype(F32)
        half = QUAD * rows // 2
        ks = split[pl.ds(0, half, stride=2), :].astype(BF16)
        vs = split[pl.ds(1, half, stride=2), :].astype(BF16)
        s = lax.dot_general(queries[...], ks, nt, preferred_element_type=F32) * scale
        new = jnp.maximum(top, jnp.max(s, axis=-1, keepdims=True))
        fade = jnp.exp(top - new)
        w = jnp.exp(s - new)
        tot = tot * fade + jnp.sum(w, axis=-1, keepdims=True)
        acc = acc * fade + jnp.dot(w.astype(BF16), vs, preferred_element_type=F32)
        return new, tot, acc

    @pl.when(is_end)
    def _():
        for m in range(PIECES):
            arrive(m)
            forward(m, near)

    for t in range(PIECES + 1):
        if t < PIECES:

            @pl.when(jnp.logical_not(is_end))
            def _():
                arrive(t)
                chain_copy(t, near).wait_recv()
                forward(t, near)

        if t > 0:
            chain_copy(t - 1, 1 - near).wait_recv()

            @pl.when(jnp.logical_not(is_end))
            def _():
                forward(t - 1, 1 - near)

            hand_out(t - 1)
        if t > 1:
            top, tot, acc = attend(t - 2, top, tot, acc)
    top, tot, acc = attend(PIECES - 1, top, tot, acc)

    mixed = acc / tot
    slot = lax.broadcasted_iota(jnp.int32, mixed.shape, 0) % cap
    mixed = jnp.where(slot < length_ref[0], mixed, 0.0).astype(BF16)
    for h in range(heads):
        att_all[tp, :, pl.ds(h * HD, HD)] = mixed[h * cap : (h + 1) * cap, :]
    attc = []
    for d in range(1, n_tp):
        c = pltpu.make_async_remote_copy(
            src_ref=att_all.at[tp],
            dst_ref=att_all.at[tp],
            send_sem=att_send.at[d - 1],
            recv_sem=att_recv.at[d - 1],
            device_id=(req, (tp + d) % n_tp),
            device_id_type=MESH,
        )
        c.start()
        attc.append(c)
    for f in fetches[4:]:
        f.wait()
    width = out_ref.shape[1]
    tile = 640 if width % 640 == 0 else width
    for d in range(n_tp):
        t = (tp + n_tp - d) % n_tp
        if d > 0:
            attc[d - 1].wait_recv()
        a = att_all[t]
        wrows = pl.ds(pl.multiple_of(t * feats, feats), feats)
        for n in range(width // tile):
            cols = pl.ds(n * tile, tile)
            part = jnp.dot(a, w_in[wrows, cols], preferred_element_type=F32)
            if d == 0:
                part = part + res_in[:, cols].astype(F32)
            else:
                part = part + total_ref[:, cols]
            if d < n_tp - 1:
                total_ref[:, cols] = part
            else:
                out_ref[:, cols] = part.astype(out_ref.dtype)

    for g in gcopies:
        g.wait_send()
    for line in first + last:
        for c in line:
            c.wait_send()
    for m in range(PIECES):
        for d in (0, 1):

            @pl.when(has_target(d))
            def _():
                chain_copy(m, d).wait_send()

    for c in attc:
        c.wait_send()


def body(
    n_req,
    n_tp,
    q_proj,
    kv_proj,
    q_bias,
    kv_bias,
    prefix_kv,
    lengths,
    group_of,
    owner,
    positions,
    residual,
    out_weight,
):
    cap, feats = q_proj.shape[1:]
    total = prefix_kv.shape[1] * 2
    rows = total // (QUAD * PIECES)
    groups = owner.shape[0]
    width = residual.shape[2]
    smem = pl.BlockSpec(memory_space=pltpu.SMEM)
    anym = pl.BlockSpec(memory_space=pl.ANY)
    dma = pltpu.SemaphoreType.DMA

    out = pl.pallas_call(
        functools.partial(kernel, n_req, n_tp, groups),
        out_shape=jax.ShapeDtypeStruct((cap, width), BF16),
        in_specs=[smem] * 4 + [anym] * 7,
        out_specs=pl.BlockSpec(memory_space=pltpu.VMEM),
        scratch_shapes=[
            pltpu.VMEM((cap, feats), BF16),
            pltpu.VMEM((2 * cap, HD), BF16),
            pltpu.VMEM((feats,), BF16),
            pltpu.VMEM((2, HD), BF16),
            pltpu.VMEM((cap, width), BF16),
            pltpu.VMEM(out_weight.shape, BF16),
            pltpu.VMEM((feats, HD), BF16),
            pltpu.VMEM((max(2 * cap, QUAD * rows), HD), F32),
            pltpu.VMEM((8, 128), jnp.int32),
            pltpu.VMEM((QUAD - 1, 8, 128), jnp.int32),
            pltpu.SMEM((QUAD - 1, 8, 128), jnp.int32),
            pltpu.VMEM((n_tp, cap, feats), BF16),
            pltpu.VMEM((cap, width), F32),
            [pltpu.VMEM((QUAD, rows, HD), BF16)] * PIECES,
            [pltpu.VMEM((2, groups, rows, HD), BF16)] * PIECES,
            [pltpu.VMEM((2, groups, rows, HD), BF16)] * PIECES,
            [pltpu.VMEM((QUAD - 1, rows, HD), BF16)] * PIECES,
            [pltpu.VMEM((QUAD, rows, HD), BF16)] * PIECES,
            dma((7 + PIECES,)),
            dma((PIECES, QUAD - 1)),
            dma((PIECES, QUAD - 1)),
            dma((PIECES, 2)),
            dma((PIECES, 2)),
            dma((PIECES, QUAD - 1)),
            dma((PIECES, QUAD - 1)),
            dma((QUAD - 1,)),
            dma((QUAD - 1,)),
            dma((max(n_tp - 1, 1),)),
            dma((max(n_tp - 1, 1),)),
        ],
        compiler_params=pltpu.CompilerParams(
            collective_id=0, has_side_effects=True, vmem_limit_bytes=60 * 1024 * 1024
        ),
        cost_estimate=pl.CostEstimate(
            flops=2 * cap * out_weight.shape[0] * width + 4 * cap * feats * (total // 2 + cap),
            bytes_accessed=2 * (out_weight.size + 2 * cap * width + total * HD),
            transcendentals=cap * feats // HD * (total // 2 + cap),
        ),
    )(
        lengths,
        group_of,
        owner,
        positions,
        q_proj[0],
        kv_proj[0].reshape(2 * cap, HD),
        q_bias,
        kv_bias,
        prefix_kv[0].reshape(total, HD),
        residual[0],
        out_weight,
    )
    return out[None]


def solution(mesh):
    in_specs = (
        P("req", None, "tp"),
        P("req", None, None, "tp"),
        P("tp"),
        P(None, "tp"),
        P("req", None, None, "tp"),
        P("req"),
        P("req"),
        P(),
        P("req", None),
        P("req", None, "tp"),
        P(None, "tp"),
    )
    out_specs = P("req", None, "tp")
    run = functools.partial(body, mesh.shape["req"], mesh.shape["tp"])
    return jax.shard_map(run, mesh=mesh, in_specs=in_specs, out_specs=out_specs, check_vma=False)
```

```python
import functools
import math

import jax
import jax.numpy as jnp
from jax import lax
from jax.experimental import pallas as pl
from jax.experimental.pallas import tpu as pltpu
from jax.sharding import PartitionSpec as P

HD = 128
QUAD = 4
PIECES = 8
MESH = pl.DeviceIdType.MESH
BF16 = jnp.bfloat16
F32 = jnp.float32


def kernel(
    n_req,
    n_tp,
    groups,
    length_ref,
    group_ref,
    owner_ref,
    pos_ref,
    q_hbm,
    kv_hbm,
    qb_hbm,
    kvb_hbm,
    slab_hbm,
    res_hbm,
    w_hbm,
    out_ref,
    q_in,
    kv_in,
    qb_in,
    kvb_in,
    res_in,
    w_in,
    queries,
    split,
    top_ref,
    tot_ref,
    acc_ref,
    gsend,
    grecv,
    gsmem,
    att_all,
    total_ref,
    p1,
    chain,
    fwd,
    outp,
    kvp,
    local_sem,
    p1_send,
    p1_recv,
    ch_send,
    ch_recv,
    p3_send,
    p3_recv,
    g_send,
    g_recv,
    att_send,
    att_recv,
):
    req = lax.axis_index("req")
    tp = lax.axis_index("tp")
    depth = n_req // QUAD
    k = req // QUAD
    q = req % QUAD
    base = k * QUAD
    rows = p1[0].shape[1]
    cap = q_in.shape[0]
    heads = q_in.shape[1] // HD
    feats = q_in.shape[1]

    def mate(d):
        return base + (q + d) % QUAD

    fetches = []
    for i, (src, dst) in enumerate(
        ((q_hbm, q_in), (kv_hbm, kv_in), (qb_hbm, qb_in), (kvb_hbm, kvb_in), (res_hbm, res_in), (w_hbm, w_in))
    ):
        fetches.append(pltpu.make_async_copy(src, dst, local_sem.at[i]))
    for f in fetches[:4]:
        f.start()

    barrier = pltpu.get_barrier_semaphore()
    for d in range(1, QUAD):
        pl.semaphore_signal(barrier, inc=1, device_id=(mate(d), tp), device_id_type=MESH)
    for d in range(1, n_tp):
        pl.semaphore_signal(barrier, inc=1, device_id=(req, (tp + d) % n_tp), device_id_type=MESH)

    @pl.when(k > 0)
    def _():
        pl.semaphore_signal(barrier, inc=1, device_id=(req - QUAD, tp), device_id_type=MESH)

    @pl.when(k < depth - 1)
    def _():
        pl.semaphore_signal(barrier, inc=1, device_id=(req + QUAD, tp), device_id_type=MESH)

    gsend[...] = jnp.full(gsend.shape, group_ref[0], jnp.int32)
    ends = jnp.where(k > 0, 1, 0) + jnp.where(k < depth - 1, 1, 0)
    pl.semaphore_wait(barrier, QUAD - 1 + n_tp - 1 + ends)

    gcopies = []
    for d in range(1, QUAD):
        c = pltpu.make_async_remote_copy(
            src_ref=gsend,
            dst_ref=grecv.at[d - 1],
            send_sem=g_send.at[d - 1],
            recv_sem=g_recv.at[d - 1],
            device_id=(mate(d), tp),
            device_id_type=MESH,
        )
        gcopies.append(c)

    first, own = [], []
    for m in range(PIECES):
        line = []
        for d in range(1, QUAD):
            to = (q + d) % QUAD
            start = pl.multiple_of((to * PIECES + m) * rows, rows)
            c = pltpu.make_async_remote_copy(
                src_ref=slab_hbm.at[pl.ds(start, rows)],
                dst_ref=p1[m].at[q],
                send_sem=p1_send.at[m, d - 1],
                recv_sem=p1_recv.at[m, d - 1],
                device_id=(mate(d), tp),
                device_id_type=MESH,
            )
            c.start()
            line.append(c)
        start = pl.multiple_of((q * PIECES + m) * rows, rows)
        c = pltpu.make_async_copy(slab_hbm.at[pl.ds(start, rows)], p1[m].at[q], local_sem.at[6 + m])
        c.start()
        own.append(c)
        first.append(line)
        if m == 0:
            for g in gcopies:
                g.start()
    for f in fetches[4:]:
        f.start()

    near = jnp.where(k < depth // 2, 0, 1)

    def chain_copy(m, d):
        step = 1 - 2 * d
        return pltpu.make_async_remote_copy(
            src_ref=fwd[m].at[d],
            dst_ref=chain[m].at[d],
            send_sem=ch_send.at[m, d],
            recv_sem=ch_recv.at[m, d],
            device_id=(req + step * QUAD, tp),
            device_id_type=MESH,
        )

    def has_target(d):
        return jnp.where(d == 0, depth - 1 - k, k) > 0

    is_end = jnp.logical_or(k == 0, k == depth - 1)
    def arrive(m):
        for c in first[m]:
            c.wait_recv()
        own[m].wait()

    def forward(m, d):
        for c in range(groups):
            o = owner_ref[c]
            mine = p1[m][o % QUAD]
            fwd[m][d, c] = jnp.where(o // QUAD == k, mine, chain[m][d, c])
        chain_copy(m, d).start()

    @pl.when(is_end)
    def _():
        for m in range(PIECES):
            arrive(m)
            forward(m, near)

    for f in fetches[:4]:
        f.wait()
    lane = lax.broadcasted_iota(jnp.int32, (cap, HD), 1)
    place = (pos_ref[0, 0] + lax.broadcasted_iota(jnp.int32, (cap, HD), 0)).astype(F32)
    index = (lane % (HD // 2)).astype(F32)
    freqs = jnp.exp(index * (-2.0 / HD) * math.log(1000000.0))
    angles = place * freqs
    cosine = jnp.cos(angles)
    sine = jnp.sin(angles)
    sine = jnp.where(lane < HD // 2, -sine, sine)

    def rot(x):
        return x * cosine + pltpu.roll(x, HD // 2, 1) * sine

    for h in range(heads):
        cols = pl.ds(h * HD, HD)
        x = q_in[:, cols].astype(F32) + qb_in[cols].astype(F32)[None, :]
        queries[pl.ds(h * cap, cap), :] = rot(x).astype(BF16)
    split[pl.ds(0, 2 * cap), :] = kv_in[...].astype(F32)
    bias = kvb_in[...].astype(F32)
    keys = rot(split[pl.ds(0, cap, stride=2), :] + bias[0:1, :]).astype(BF16)
    vals = (split[pl.ds(1, cap, stride=2), :] + bias[1:2, :]).astype(BF16)
    scale = 1.0 / math.sqrt(HD)
    nt = (((1,), (1,)), ((), ()))

    qs = queries[...]
    s = lax.dot_general(qs, keys, nt, preferred_element_type=F32) * scale
    seen = lax.broadcasted_iota(jnp.int32, s.shape, 1) <= lax.broadcasted_iota(jnp.int32, s.shape, 0) % cap
    s = jnp.where(seen, s, -1e30)
    top = jnp.max(s, axis=-1, keepdims=True)
    w = jnp.where(seen, jnp.exp(s - top), 0.0)
    top_ref[...] = top
    tot_ref[...] = jnp.sum(w, axis=-1, keepdims=True)
    acc_ref[...] = jnp.dot(w.astype(BF16), vals, preferred_element_type=F32)

    for d in range(1, QUAD):
        gcopies[d - 1].wait_recv()
    to_smem = pltpu.make_async_copy(grecv, gsmem, local_sem.at[6 + PIECES])
    to_smem.start()
    to_smem.wait()
    wants = [group_ref[0]]
    for d in range(1, QUAD):
        wants.append(gsmem[QUAD - d - 1, 0, 0])

    last = []

    def hand_out(m):
        line = []
        for d in (1, 2, 3, 0):
            c = wants[d]
            o = owner_ref[c]
            oz = o // QUAD
            other = jnp.where(oz < k, chain[m][0, c], chain[m][1, c])
            piece = jnp.where(oz == k, p1[m][o % QUAD], other)
            if d == 0:
                kvp[m][q] = piece
            else:
                outp[m][d - 1] = piece
                r = pltpu.make_async_remote_copy(
                    src_ref=outp[m].at[d - 1],
                    dst_ref=kvp[m].at[q],
                    send_sem=p3_send.at[m, d - 1],
                    recv_sem=p3_recv.at[m, d - 1],
                    device_id=(mate(d), tp),
                    device_id_type=MESH,
                )
                r.start()
                line.append(r)
        last.append(line)

    def attend(pieces):
        span = QUAD * rows
        for i, m in enumerate(pieces):
            for r in last[m]:
                r.wait_recv()
            for j in range(QUAD):
                split[pl.ds(i * span + j * rows, rows), :] = kvp[m][j].astype(F32)
        half = len(pieces) * span // 2
        ks = split[pl.ds(0, half, stride=2), :].astype(BF16)
        vs = split[pl.ds(1, half, stride=2), :].astype(BF16)
        s = lax.dot_general(queries[...], ks, nt, preferred_element_type=F32) * scale
        top = top_ref[...]
        new = jnp.maximum(top, jnp.max(s, axis=-1, keepdims=True))
        fade = jnp.exp(top - new)
        w = jnp.exp(s - new)
        top_ref[...] = new
        tot_ref[...] = tot_ref[...] * fade + jnp.sum(w, axis=-1, keepdims=True)
        acc_ref[...] = acc_ref[...] * fade + jnp.dot(w.astype(BF16), vs, preferred_element_type=F32)

    early = {t: [t - 3, t - 2] for t in range(3, PIECES, 2)}
    early[PIECES] = [PIECES - 2]
    for t in range(PIECES + 1):
        if t < PIECES:

            @pl.when(jnp.logical_not(is_end))
            def _():
                arrive(t)
                chain_copy(t, near).wait_recv()
                forward(t, near)

        if t > 0:
            chain_copy(t - 1, 1 - near).wait_recv()

            @pl.when(jnp.logical_not(is_end))
            def _():
                forward(t - 1, 1 - near)

            hand_out(t - 1)
        if t in early:

            @pl.when(is_end)
            def _():
                attend(early[t])

    @pl.when(is_end)
    def _():
        attend([PIECES - 1])

    @pl.when(jnp.logical_not(is_end))
    def _():
        for m in range(0, PIECES, 4):
            attend(range(m, m + 4))

    mixed = acc_ref[...] / tot_ref[...]
    slot = lax.broadcasted_iota(jnp.int32, mixed.shape, 0) % cap
    mixed = jnp.where(slot < length_ref[0], mixed, 0.0).astype(BF16)
    for h in range(heads):
        att_all[tp, :, pl.ds(h * HD, HD)] = mixed[h * cap : (h + 1) * cap, :]
    attc = []
    for d in range(1, n_tp):
        c = pltpu.make_async_remote_copy(
            src_ref=att_all.at[tp],
            dst_ref=att_all.at[tp],
            send_sem=att_send.at[d - 1],
            recv_sem=att_recv.at[d - 1],
            device_id=(req, (tp + d) % n_tp),
            device_id_type=MESH,
        )
        c.start()
        attc.append(c)
    for f in fetches[4:]:
        f.wait()
    width = out_ref.shape[1]
    tile = 640 if width % 640 == 0 else width
    for d in range(n_tp):
        t = (tp + n_tp - d) % n_tp
        if d > 0:
            attc[d - 1].wait_recv()
        a = att_all[t]
        wrows = pl.ds(pl.multiple_of(t * feats, feats), feats)
        for n in range(width // tile):
            cols = pl.ds(n * tile, tile)
            part = jnp.dot(a, w_in[wrows, cols], preferred_element_type=F32)
            if d == 0:
                part = part + res_in[:, cols].astype(F32)
            else:
                part = part + total_ref[:, cols]
            if d < n_tp - 1:
                total_ref[:, cols] = part
            else:
                out_ref[:, cols] = part.astype(out_ref.dtype)

    for g in gcopies:
        g.wait_send()
    for line in first + last:
        for c in line:
            c.wait_send()
    for m in range(PIECES):
        for d in (0, 1):

            @pl.when(has_target(d))
            def _():
                chain_copy(m, d).wait_send()

    for c in attc:
        c.wait_send()


def body(
    n_req,
    n_tp,
    q_proj,
    kv_proj,
    q_bias,
    kv_bias,
    prefix_kv,
    lengths,
    group_of,
    owner,
    positions,
    residual,
    out_weight,
):
    cap, feats = q_proj.shape[1:]
    total = prefix_kv.shape[1] * 2
    rows = total // (QUAD * PIECES)
    groups = owner.shape[0]
    width = residual.shape[2]
    smem = pl.BlockSpec(memory_space=pltpu.SMEM)
    anym = pl.BlockSpec(memory_space=pl.ANY)
    dma = pltpu.SemaphoreType.DMA

    out = pl.pallas_call(
        functools.partial(kernel, n_req, n_tp, groups),
        out_shape=jax.ShapeDtypeStruct((cap, width), BF16),
        in_specs=[smem] * 4 + [anym] * 7,
        out_specs=pl.BlockSpec(memory_space=pltpu.VMEM),
        scratch_shapes=[
            pltpu.VMEM((cap, feats), BF16),
            pltpu.VMEM((2 * cap, HD), BF16),
            pltpu.VMEM((feats,), BF16),
            pltpu.VMEM((2, HD), BF16),
            pltpu.VMEM((cap, width), BF16),
            pltpu.VMEM(out_weight.shape, BF16),
            pltpu.VMEM((feats, HD), BF16),
            pltpu.VMEM((max(2 * cap, 4 * QUAD * rows), HD), F32),
            pltpu.VMEM((feats, 1), F32),
            pltpu.VMEM((feats, 1), F32),
            pltpu.VMEM((feats, HD), F32),
            pltpu.VMEM((8, 128), jnp.int32),
            pltpu.VMEM((QUAD - 1, 8, 128), jnp.int32),
            pltpu.SMEM((QUAD - 1, 8, 128), jnp.int32),
            pltpu.VMEM((n_tp, cap, feats), BF16),
            pltpu.VMEM((cap, width), F32),
            [pltpu.VMEM((QUAD, rows, HD), BF16)] * PIECES,
            [pltpu.VMEM((2, groups, rows, HD), BF16)] * PIECES,
            [pltpu.VMEM((2, groups, rows, HD), BF16)] * PIECES,
            [pltpu.VMEM((QUAD - 1, rows, HD), BF16)] * PIECES,
            [pltpu.VMEM((QUAD, rows, HD), BF16)] * PIECES,
            dma((7 + PIECES,)),
            dma((PIECES, QUAD - 1)),
            dma((PIECES, QUAD - 1)),
            dma((PIECES, 2)),
            dma((PIECES, 2)),
            dma((PIECES, QUAD - 1)),
            dma((PIECES, QUAD - 1)),
            dma((QUAD - 1,)),
            dma((QUAD - 1,)),
            dma((max(n_tp - 1, 1),)),
            dma((max(n_tp - 1, 1),)),
        ],
        compiler_params=pltpu.CompilerParams(
            collective_id=0, has_side_effects=True, vmem_limit_bytes=60 * 1024 * 1024
        ),
        cost_estimate=pl.CostEstimate(
            flops=2 * cap * out_weight.shape[0] * width + 4 * cap * feats * (total // 2 + cap),
            bytes_accessed=2 * (out_weight.size + 2 * cap * width + total * HD),
            transcendentals=cap * feats // HD * (total // 2 + cap),
        ),
    )(
        lengths,
        group_of,
        owner,
        positions,
        q_proj[0],
        kv_proj[0].reshape(2 * cap, HD),
        q_bias,
        kv_bias,
        prefix_kv[0].reshape(total, HD),
        residual[0],
        out_weight,
    )
    return out[None]


def solution(mesh):
    in_specs = (
        P("req", None, "tp"),
        P("req", None, None, "tp"),
        P("tp"),
        P(None, "tp"),
        P("req", None, None, "tp"),
        P("req"),
        P("req"),
        P(),
        P("req", None),
        P("req", None, "tp"),
        P(None, "tp"),
    )
    out_specs = P("req", None, "tp")
    run = functools.partial(body, mesh.shape["req"], mesh.shape["tp"])
    return jax.shard_map(run, mesh=mesh, in_specs=in_specs, out_specs=out_specs, check_vma=False)
```

```python
import functools
import math

import jax
import jax.numpy as jnp
from jax import lax
from jax.experimental import pallas as pl
from jax.experimental.pallas import tpu as pltpu
from jax.sharding import PartitionSpec as P

HD = 128
QUAD = 4
PIECES = 4
MESH = pl.DeviceIdType.MESH
BF16 = jnp.bfloat16
F32 = jnp.float32


def kernel(
    n_req,
    n_tp,
    groups,
    length_ref,
    group_ref,
    owner_ref,
    pos_ref,
    q_hbm,
    kv_hbm,
    qb_hbm,
    kvb_hbm,
    slab_hbm,
    att_all,
    q_in,
    kv_in,
    qb_in,
    kvb_in,
    queries,
    split,
    top_ref,
    tot_ref,
    acc_ref,
    gsend,
    grecv,
    gsmem,
    p1,
    chain,
    fwd,
    outp,
    kvp,
    local_sem,
    p1_send,
    p1_recv,
    ch_send,
    ch_recv,
    p3_send,
    p3_recv,
    g_send,
    g_recv,
    att_send,
    att_recv,
):
    req = lax.axis_index("req")
    tp = lax.axis_index("tp")
    depth = n_req // QUAD
    k = req // QUAD
    q = req % QUAD
    base = k * QUAD
    rows = p1[0].shape[1]
    cap = q_in.shape[0]
    heads = q_in.shape[1] // HD
    feats = q_in.shape[1]

    def mate(d):
        return base + (q + d) % QUAD

    fetches = []
    for i, (src, dst) in enumerate(
        ((q_hbm, q_in), (kv_hbm, kv_in), (qb_hbm, qb_in), (kvb_hbm, kvb_in))
    ):
        fetches.append(pltpu.make_async_copy(src, dst, local_sem.at[i]))
    for f in fetches:
        f.start()

    barrier = pltpu.get_barrier_semaphore()
    for d in range(1, QUAD):
        pl.semaphore_signal(barrier, inc=1, device_id=(mate(d), tp), device_id_type=MESH)
    for d in range(1, n_tp):
        pl.semaphore_signal(barrier, inc=1, device_id=(req, (tp + d) % n_tp), device_id_type=MESH)

    @pl.when(k > 0)
    def _():
        pl.semaphore_signal(barrier, inc=1, device_id=(req - QUAD, tp), device_id_type=MESH)

    @pl.when(k < depth - 1)
    def _():
        pl.semaphore_signal(barrier, inc=1, device_id=(req + QUAD, tp), device_id_type=MESH)

    gsend[...] = jnp.full(gsend.shape, group_ref[0], jnp.int32)
    ends = jnp.where(k > 0, 1, 0) + jnp.where(k < depth - 1, 1, 0)
    pl.semaphore_wait(barrier, QUAD - 1 + n_tp - 1 + ends)

    gcopies = []
    for d in range(1, QUAD):
        c = pltpu.make_async_remote_copy(
            src_ref=gsend,
            dst_ref=grecv.at[d - 1],
            send_sem=g_send.at[d - 1],
            recv_sem=g_recv.at[d - 1],
            device_id=(mate(d), tp),
            device_id_type=MESH,
        )
        gcopies.append(c)

    first, own = [], []
    for m in range(PIECES):
        line = []
        for d in range(1, QUAD):
            to = (q + d) % QUAD
            start = pl.multiple_of((to * PIECES + m) * rows, rows)
            c = pltpu.make_async_remote_copy(
                src_ref=slab_hbm.at[pl.ds(start, rows)],
                dst_ref=p1[m].at[q],
                send_sem=p1_send.at[m, d - 1],
                recv_sem=p1_recv.at[m, d - 1],
                device_id=(mate(d), tp),
                device_id_type=MESH,
            )
            line.append(c)
        start = pl.multiple_of((q * PIECES + m) * rows, rows)
        c = pltpu.make_async_copy(slab_hbm.at[pl.ds(start, rows)], p1[m].at[q], local_sem.at[6 + m])
        own.append(c)
        first.append(line)

    def depart(m):
        if m < PIECES:
            for c in first[m] + [own[m]]:
                c.start()

    depart(0)
    for g in gcopies:
        g.start()
    depart(1)

    near = jnp.where(k < depth // 2, 0, 1)

    def chain_copy(m, d):
        step = 1 - 2 * d
        return pltpu.make_async_remote_copy(
            src_ref=fwd[m].at[d],
            dst_ref=chain[m].at[d],
            send_sem=ch_send.at[m, d],
            recv_sem=ch_recv.at[m, d],
            device_id=(req + step * QUAD, tp),
            device_id_type=MESH,
        )

    def has_target(d):
        return jnp.where(d == 0, depth - 1 - k, k) > 0

    is_end = jnp.logical_or(k == 0, k == depth - 1)
    def arrive(m):
        for c in first[m]:
            c.wait_recv()
        own[m].wait()

    def forward(m, d):
        for c in range(groups):
            o = owner_ref[c]
            mine = p1[m][o % QUAD]
            fwd[m][d, c] = jnp.where(o // QUAD == k, mine, chain[m][d, c])
        chain_copy(m, d).start()

    @pl.when(is_end)
    def _():
        for m in range(PIECES):
            arrive(m)
            depart(m + 2)
            forward(m, near)

    for f in fetches:
        f.wait()
    lane = lax.broadcasted_iota(jnp.int32, (cap, HD), 1)
    place = (pos_ref[0, 0] + lax.broadcasted_iota(jnp.int32, (cap, HD), 0)).astype(F32)
    index = (lane % (HD // 2)).astype(F32)
    freqs = jnp.exp(index * (-2.0 / HD) * math.log(1000000.0))
    angles = place * freqs
    cosine = jnp.cos(angles)
    sine = jnp.sin(angles)
    sine = jnp.where(lane < HD // 2, -sine, sine)

    def rot(x):
        return x * cosine + pltpu.roll(x, HD // 2, 1) * sine

    for h in range(heads):
        cols = pl.ds(h * HD, HD)
        x = q_in[:, cols].astype(F32) + qb_in[cols].astype(F32)[None, :]
        queries[pl.ds(h * cap, cap), :] = rot(x).astype(BF16)
    split[pl.ds(0, 2 * cap), :] = kv_in[...].astype(F32)
    bias = kvb_in[...].astype(F32)
    keys = rot(split[pl.ds(0, cap, stride=2), :] + bias[0:1, :]).astype(BF16)
    vals = (split[pl.ds(1, cap, stride=2), :] + bias[1:2, :]).astype(BF16)
    scale = 1.0 / math.sqrt(HD)
    nt = (((1,), (1,)), ((), ()))

    qs = queries[...]
    s = lax.dot_general(qs, keys, nt, preferred_element_type=F32) * scale
    seen = lax.broadcasted_iota(jnp.int32, s.shape, 1) <= lax.broadcasted_iota(jnp.int32, s.shape, 0) % cap
    s = jnp.where(seen, s, -1e30)
    top = jnp.max(s, axis=-1, keepdims=True)
    w = jnp.where(seen, jnp.exp(s - top), 0.0)
    top_ref[...] = top
    tot_ref[...] = jnp.sum(w, axis=-1, keepdims=True)
    acc_ref[...] = jnp.dot(w.astype(BF16), vals, preferred_element_type=F32)

    for d in range(1, QUAD):
        gcopies[d - 1].wait_recv()
    to_smem = pltpu.make_async_copy(grecv, gsmem, local_sem.at[6 + PIECES])
    to_smem.start()
    to_smem.wait()
    wants = [group_ref[0]]
    for d in range(1, QUAD):
        wants.append(gsmem[QUAD - d - 1, 0, 0])

    last = []

    def hand_out(m):
        line = []
        for d in (1, 2, 3, 0):
            c = wants[d]
            o = owner_ref[c]
            oz = o // QUAD
            other = jnp.where(oz < k, chain[m][0, c], chain[m][1, c])
            piece = jnp.where(oz == k, p1[m][o % QUAD], other)
            if d == 0:
                kvp[m][q] = piece
            else:
                outp[m][d - 1] = piece
                r = pltpu.make_async_remote_copy(
                    src_ref=outp[m].at[d - 1],
                    dst_ref=kvp[m].at[q],
                    send_sem=p3_send.at[m, d - 1],
                    recv_sem=p3_recv.at[m, d - 1],
                    device_id=(mate(d), tp),
                    device_id_type=MESH,
                )
                r.start()
                line.append(r)
        last.append(line)

    def attend(pieces):
        span = QUAD * rows
        for i, m in enumerate(pieces):
            for r in last[m]:
                r.wait_recv()
            for j in range(QUAD):
                split[pl.ds(i * span + j * rows, rows), :] = kvp[m][j].astype(F32)
        half = len(pieces) * span // 2
        ks = split[pl.ds(0, half, stride=2), :].astype(BF16)
        vs = split[pl.ds(1, half, stride=2), :].astype(BF16)
        s = lax.dot_general(queries[...], ks, nt, preferred_element_type=F32) * scale
        top = top_ref[...]
        new = jnp.maximum(top, jnp.max(s, axis=-1, keepdims=True))
        fade = jnp.exp(top - new)
        w = jnp.exp(s - new)
        top_ref[...] = new
        tot_ref[...] = tot_ref[...] * fade + jnp.sum(w, axis=-1, keepdims=True)
        acc_ref[...] = acc_ref[...] * fade + jnp.dot(w.astype(BF16), vs, preferred_element_type=F32)

    early = {t: [t - 2] for t in range(2, PIECES + 1)}
    for t in range(PIECES + 1):
        if t < PIECES:

            @pl.when(jnp.logical_not(is_end))
            def _():
                arrive(t)
                depart(t + 2)
                chain_copy(t, near).wait_recv()
                forward(t, near)

        if t > 0:
            chain_copy(t - 1, 1 - near).wait_recv()

            @pl.when(jnp.logical_not(is_end))
            def _():
                forward(t - 1, 1 - near)

            hand_out(t - 1)
        if t in early:

            @pl.when(is_end)
            def _():
                attend(early[t])

    @pl.when(is_end)
    def _():
        attend([PIECES - 1])

    @pl.when(jnp.logical_not(is_end))
    def _():
        for m in range(0, PIECES, 2):
            attend(range(m, m + 2))

    mixed = acc_ref[...] / tot_ref[...]
    slot = lax.broadcasted_iota(jnp.int32, mixed.shape, 0) % cap
    mixed = jnp.where(slot < length_ref[0], mixed, 0.0).astype(BF16)
    for h in range(heads):
        att_all[tp, :, pl.ds(h * HD, HD)] = mixed[h * cap : (h + 1) * cap, :]
    attc = []
    for d in range(1, n_tp):
        c = pltpu.make_async_remote_copy(
            src_ref=att_all.at[tp],
            dst_ref=att_all.at[tp],
            send_sem=att_send.at[d - 1],
            recv_sem=att_recv.at[d - 1],
            device_id=(req, (tp + d) % n_tp),
            device_id_type=MESH,
        )
        c.start()
        attc.append(c)
    for c in attc:
        c.wait_recv()

    for g in gcopies:
        g.wait_send()
    for line in first + last:
        for c in line:
            c.wait_send()
    for m in range(PIECES):
        for d in (0, 1):

            @pl.when(has_target(d))
            def _():
                chain_copy(m, d).wait_send()

    for c in attc:
        c.wait_send()


def project(n_tp, att_ref, w_ref, res_ref, out_ref):
    feats = att_ref.shape[2]
    total = res_ref[...].astype(F32)
    for t in range(n_tp):
        total = total + jnp.dot(att_ref[t], w_ref[pl.ds(t * feats, feats), :], preferred_element_type=F32)
    out_ref[...] = total.astype(BF16)


def body(
    n_req,
    n_tp,
    q_proj,
    kv_proj,
    q_bias,
    kv_bias,
    prefix_kv,
    lengths,
    group_of,
    owner,
    positions,
    residual,
    out_weight,
):
    cap, feats = q_proj.shape[1:]
    total = prefix_kv.shape[1] * 2
    rows = total // (QUAD * PIECES)
    groups = owner.shape[0]
    width = residual.shape[2]
    smem = pl.BlockSpec(memory_space=pltpu.SMEM)
    anym = pl.BlockSpec(memory_space=pl.ANY)
    dma = pltpu.SemaphoreType.DMA

    att = pl.pallas_call(
        functools.partial(kernel, n_req, n_tp, groups),
        out_shape=jax.ShapeDtypeStruct((n_tp, cap, feats), BF16),
        in_specs=[smem] * 4 + [anym] * 5,
        out_specs=pl.BlockSpec(memory_space=pltpu.VMEM),
        scratch_shapes=[
            pltpu.VMEM((cap, feats), BF16),
            pltpu.VMEM((2 * cap, HD), BF16),
            pltpu.VMEM((feats,), BF16),
            pltpu.VMEM((2, HD), BF16),
            pltpu.VMEM((feats, HD), BF16),
            pltpu.VMEM((max(2 * cap, 2 * QUAD * rows), HD), F32),
            pltpu.VMEM((feats, 1), F32),
            pltpu.VMEM((feats, 1), F32),
            pltpu.VMEM((feats, HD), F32),
            pltpu.VMEM((8, 128), jnp.int32),
            pltpu.VMEM((QUAD - 1, 8, 128), jnp.int32),
            pltpu.SMEM((QUAD - 1, 8, 128), jnp.int32),
            [pltpu.VMEM((QUAD, rows, HD), BF16)] * PIECES,
            [pltpu.VMEM((2, groups, rows, HD), BF16)] * PIECES,
            [pltpu.VMEM((2, groups, rows, HD), BF16)] * PIECES,
            [pltpu.VMEM((QUAD - 1, rows, HD), BF16)] * PIECES,
            [pltpu.VMEM((QUAD, rows, HD), BF16)] * PIECES,
            dma((7 + PIECES,)),
            dma((PIECES, QUAD - 1)),
            dma((PIECES, QUAD - 1)),
            dma((PIECES, 2)),
            dma((PIECES, 2)),
            dma((PIECES, QUAD - 1)),
            dma((PIECES, QUAD - 1)),
            dma((QUAD - 1,)),
            dma((QUAD - 1,)),
            dma((max(n_tp - 1, 1),)),
            dma((max(n_tp - 1, 1),)),
        ],
        compiler_params=pltpu.CompilerParams(
            collective_id=0, has_side_effects=True, vmem_limit_bytes=60 * 1024 * 1024
        ),
        cost_estimate=pl.CostEstimate(
            flops=4 * cap * feats * (total // 2 + cap),
            bytes_accessed=4 * total * HD,
            transcendentals=cap * feats // HD * (total // 2 + cap),
        ),
    )(
        lengths,
        group_of,
        owner,
        positions,
        q_proj[0],
        kv_proj[0].reshape(2 * cap, HD),
        q_bias,
        kv_bias,
        prefix_kv[0].reshape(total, HD),
    )
    tile = 640 if width % 640 == 0 else width
    out = pl.pallas_call(
        functools.partial(project, n_tp),
        grid=(width // tile,),
        out_shape=jax.ShapeDtypeStruct((cap, width), BF16),
        in_specs=[
            pl.BlockSpec((n_tp, cap, feats), lambda n: (0, 0, 0)),
            pl.BlockSpec((n_tp * feats, tile), lambda n: (0, n)),
            pl.BlockSpec((cap, tile), lambda n: (0, n)),
        ],
        out_specs=pl.BlockSpec((cap, tile), lambda n: (0, n)),
        compiler_params=pltpu.CompilerParams(vmem_limit_bytes=60 * 1024 * 1024),
        cost_estimate=pl.CostEstimate(
            flops=2 * cap * out_weight.shape[0] * width,
            bytes_accessed=2 * (out_weight.size + 2 * cap * width),
            transcendentals=0,
        ),
    )(att, out_weight, residual[0])
    return out[None]


def solution(mesh):
    in_specs = (
        P("req", None, "tp"),
        P("req", None, None, "tp"),
        P("tp"),
        P(None, "tp"),
        P("req", None, None, "tp"),
        P("req"),
        P("req"),
        P(),
        P("req", None),
        P("req", None, "tp"),
        P(None, "tp"),
    )
    out_specs = P("req", None, "tp")
    run = functools.partial(body, mesh.shape["req"], mesh.shape["tp"])
    return jax.shard_map(run, mesh=mesh, in_specs=in_specs, out_specs=out_specs, check_vma=False)
```

```python
import functools
import math

import jax
import jax.numpy as jnp
from jax import lax
from jax.experimental import pallas as pl
from jax.experimental.pallas import tpu as pltpu
from jax.sharding import PartitionSpec as P

HD = 128
QUAD = 4
PIECES = 4
MESH = pl.DeviceIdType.MESH
BF16 = jnp.bfloat16
F32 = jnp.float32


def kernel(
    n_req,
    n_tp,
    groups,
    length_ref,
    group_ref,
    owner_ref,
    pos_ref,
    q_hbm,
    kv_hbm,
    qb_hbm,
    kvb_hbm,
    slab_hbm,
    res_hbm,
    w_hbm,
    out_ref,
    q_in,
    kv_in,
    qb_in,
    kvb_in,
    res_in,
    w_in,
    queries,
    split,
    top_ref,
    tot_ref,
    acc_ref,
    gsend,
    grecv,
    gsmem,
    att_all,
    total_ref,
    p1,
    chain,
    fwd,
    outp,
    kvp,
    local_sem,
    p1_send,
    p1_recv,
    ch_send,
    ch_recv,
    p3_send,
    p3_recv,
    g_send,
    g_recv,
    att_send,
    att_recv,
):
    req = lax.axis_index("req")
    tp = lax.axis_index("tp")
    depth = n_req // QUAD
    k = req // QUAD
    q = req % QUAD
    base = k * QUAD
    rows = p1[0].shape[1]
    cap = q_in.shape[0]
    heads = q_in.shape[1] // HD
    feats = q_in.shape[1]

    def mate(d):
        return base + (q + d) % QUAD

    fetches = []
    for i, (src, dst) in enumerate(
        ((q_hbm, q_in), (kv_hbm, kv_in), (qb_hbm, qb_in), (kvb_hbm, kvb_in), (res_hbm, res_in), (w_hbm, w_in))
    ):
        fetches.append(pltpu.make_async_copy(src, dst, local_sem.at[i]))
    for f in fetches[:4]:
        f.start()

    barrier = pltpu.get_barrier_semaphore()
    for d in range(1, QUAD):
        pl.semaphore_signal(barrier, inc=1, device_id=(mate(d), tp), device_id_type=MESH)
    for d in range(1, n_tp):
        pl.semaphore_signal(barrier, inc=1, device_id=(req, (tp + d) % n_tp), device_id_type=MESH)

    @pl.when(k > 0)
    def _():
        pl.semaphore_signal(barrier, inc=1, device_id=(req - QUAD, tp), device_id_type=MESH)

    @pl.when(k < depth - 1)
    def _():
        pl.semaphore_signal(barrier, inc=1, device_id=(req + QUAD, tp), device_id_type=MESH)

    gsend[...] = jnp.full(gsend.shape, group_ref[0], jnp.int32)
    ends = jnp.where(k > 0, 1, 0) + jnp.where(k < depth - 1, 1, 0)
    pl.semaphore_wait(barrier, QUAD - 1 + n_tp - 1 + ends)

    gcopies = []
    for d in range(1, QUAD):
        c = pltpu.make_async_remote_copy(
            src_ref=gsend,
            dst_ref=grecv.at[d - 1],
            send_sem=g_send.at[d - 1],
            recv_sem=g_recv.at[d - 1],
            device_id=(mate(d), tp),
            device_id_type=MESH,
        )
        gcopies.append(c)

    first, own = [], []
    for m in range(PIECES):
        line = []
        for d in range(1, QUAD):
            to = (q + d) % QUAD
            start = pl.multiple_of((to * PIECES + m) * rows, rows)
            c = pltpu.make_async_remote_copy(
                src_ref=slab_hbm.at[pl.ds(start, rows)],
                dst_ref=p1[m].at[q],
                send_sem=p1_send.at[m, d - 1],
                recv_sem=p1_recv.at[m, d - 1],
                device_id=(mate(d), tp),
                device_id_type=MESH,
            )
            line.append(c)
        start = pl.multiple_of((q * PIECES + m) * rows, rows)
        c = pltpu.make_async_copy(slab_hbm.at[pl.ds(start, rows)], p1[m].at[q], local_sem.at[6 + m])
        own.append(c)
        first.append(line)

    def depart(m):
        if m < PIECES:
            for c in first[m] + [own[m]]:
                c.start()

    depart(0)
    for g in gcopies:
        g.start()
    depart(1)
    for f in fetches[4:]:
        f.start()

    near = jnp.where(k < depth // 2, 0, 1)

    def chain_copy(m, d, c):
        step = 1 - 2 * d
        return pltpu.make_async_remote_copy(
            src_ref=fwd[m].at[d, c],
            dst_ref=chain[m].at[d, c],
            send_sem=ch_send.at[m, d * groups + c],
            recv_sem=ch_recv.at[m, d * groups + c],
            device_id=(req + step * QUAD, tp),
            device_id_type=MESH,
        )

    def has_target(d):
        return jnp.where(d == 0, depth - 1 - k, k) > 0

    is_end = jnp.logical_or(k == 0, k == depth - 1)
    def arrive(m):
        for c in first[m]:
            c.wait_recv()
        own[m].wait()

    def forward(m, d, wait):
        for c in range(groups):
            if wait:
                chain_copy(m, d, c).wait_recv()
            o = owner_ref[c]
            mine = p1[m][o % QUAD]
            fwd[m][d, c] = jnp.where(o // QUAD == k, mine, chain[m][d, c])
            chain_copy(m, d, c).start()

    @pl.when(is_end)
    def _():
        for m in range(PIECES):
            arrive(m)
            depart(m + 2)
            forward(m, near, False)

    @pl.when(jnp.logical_not(is_end))
    def _():
        for m in range(2, PIECES):
            depart(m)

    for f in fetches[:4]:
        f.wait()
    lane = lax.broadcasted_iota(jnp.int32, (cap, HD), 1)
    place = (pos_ref[0, 0] + lax.broadcasted_iota(jnp.int32, (cap, HD), 0)).astype(F32)
    index = (lane % (HD // 2)).astype(F32)
    freqs = jnp.exp(index * (-2.0 / HD) * math.log(1000000.0))
    angles = place * freqs
    cosine = jnp.cos(angles)
    sine = jnp.sin(angles)
    sine = jnp.where(lane < HD // 2, -sine, sine)

    def rot(x):
        return x * cosine + pltpu.roll(x, HD // 2, 1) * sine

    for h in range(heads):
        cols = pl.ds(h * HD, HD)
        x = q_in[:, cols].astype(F32) + qb_in[cols].astype(F32)[None, :]
        queries[pl.ds(h * cap, cap), :] = rot(x).astype(BF16)
    split[pl.ds(0, 2 * cap), :] = kv_in[...].astype(F32)
    bias = kvb_in[...].astype(F32)
    keys = rot(split[pl.ds(0, cap, stride=2), :] + bias[0:1, :]).astype(BF16)
    vals = (split[pl.ds(1, cap, stride=2), :] + bias[1:2, :]).astype(BF16)
    scale = 1.0 / math.sqrt(HD)
    nt = (((1,), (1,)), ((), ()))

    qs = queries[...]
    s = lax.dot_general(qs, keys, nt, preferred_element_type=F32) * scale
    seen = lax.broadcasted_iota(jnp.int32, s.shape, 1) <= lax.broadcasted_iota(jnp.int32, s.shape, 0) % cap
    s = jnp.where(seen, s, -1e30)
    top = jnp.max(s, axis=-1, keepdims=True)
    w = jnp.where(seen, jnp.exp(s - top), 0.0)
    top_ref[...] = top
    tot_ref[...] = jnp.sum(w, axis=-1, keepdims=True)
    acc_ref[...] = jnp.dot(w.astype(BF16), vals, preferred_element_type=F32)

    for d in range(1, QUAD):
        gcopies[d - 1].wait_recv()
    to_smem = pltpu.make_async_copy(grecv, gsmem, local_sem.at[6 + PIECES])
    to_smem.start()
    to_smem.wait()
    wants = [group_ref[0]]
    for d in range(1, QUAD):
        wants.append(gsmem[QUAD - d - 1, 0, 0])

    last = []

    def hand_out(m):
        line = []
        for d in (1, 2, 3, 0):
            c = wants[d]
            o = owner_ref[c]
            oz = o // QUAD
            other = jnp.where(oz < k, chain[m][0, c], chain[m][1, c])
            piece = jnp.where(oz == k, p1[m][o % QUAD], other)
            if d == 0:
                kvp[m][q] = piece
            else:
                outp[m][d - 1] = piece
                r = pltpu.make_async_remote_copy(
                    src_ref=outp[m].at[d - 1],
                    dst_ref=kvp[m].at[q],
                    send_sem=p3_send.at[m, d - 1],
                    recv_sem=p3_recv.at[m, d - 1],
                    device_id=(mate(d), tp),
                    device_id_type=MESH,
                )
                r.start()
                line.append(r)
        last.append(line)

    def attend(pieces):
        span = QUAD * rows
        for i, m in enumerate(pieces):
            for r in last[m]:
                r.wait_recv()
            for j in range(QUAD):
                split[pl.ds(i * span + j * rows, rows), :] = kvp[m][j].astype(F32)
        half = len(pieces) * span // 2
        ks = split[pl.ds(0, half, stride=2), :].astype(BF16)
        vs = split[pl.ds(1, half, stride=2), :].astype(BF16)
        s = lax.dot_general(queries[...], ks, nt, preferred_element_type=F32) * scale
        top = top_ref[...]
        new = jnp.maximum(top, jnp.max(s, axis=-1, keepdims=True))
        fade = jnp.exp(top - new)
        w = jnp.exp(s - new)
        top_ref[...] = new
        tot_ref[...] = tot_ref[...] * fade + jnp.sum(w, axis=-1, keepdims=True)
        acc_ref[...] = acc_ref[...] * fade + jnp.dot(w.astype(BF16), vs, preferred_element_type=F32)

    early = {t: [t - 2] for t in range(2, PIECES + 1)}
    for t in range(PIECES + 1):
        if t < PIECES:

            @pl.when(jnp.logical_not(is_end))
            def _():
                arrive(t)
                forward(t, near, True)

        if t > 0:

            @pl.when(is_end)
            def _():
                for c in range(groups):
                    chain_copy(t - 1, 1 - near, c).wait_recv()

            @pl.when(jnp.logical_not(is_end))
            def _():
                forward(t - 1, 1 - near, True)

            hand_out(t - 1)
        if t in early:

            @pl.when(is_end)
            def _():
                attend(early[t])

    @pl.when(is_end)
    def _():
        attend([PIECES - 1])

    @pl.when(jnp.logical_not(is_end))
    def _():
        for m in range(0, PIECES, 2):
            attend(range(m, m + 2))

    mixed = acc_ref[...] / tot_ref[...]
    slot = lax.broadcasted_iota(jnp.int32, mixed.shape, 0) % cap
    mixed = jnp.where(slot < length_ref[0], mixed, 0.0).astype(BF16)
    for h in range(heads):
        att_all[tp, :, pl.ds(h * HD, HD)] = mixed[h * cap : (h + 1) * cap, :]
    attc = []
    for d in range(1, n_tp):
        c = pltpu.make_async_remote_copy(
            src_ref=att_all.at[tp],
            dst_ref=att_all.at[tp],
            send_sem=att_send.at[d - 1],
            recv_sem=att_recv.at[d - 1],
            device_id=(req, (tp + d) % n_tp),
            device_id_type=MESH,
        )
        c.start()
        attc.append(c)
    for f in fetches[4:]:
        f.wait()
    width = out_ref.shape[1]
    tile = 640 if width % 640 == 0 else width
    for d in range(n_tp):
        t = (tp + n_tp - d) % n_tp
        if d > 0:
            attc[d - 1].wait_recv()
        a = att_all[t]
        wrows = pl.ds(pl.multiple_of(t * feats, feats), feats)
        for n in range(width // tile):
            cols = pl.ds(n * tile, tile)
            part = jnp.dot(a, w_in[wrows, cols], preferred_element_type=F32)
            if d == 0:
                part = part + res_in[:, cols].astype(F32)
            else:
                part = part + total_ref[:, cols]
            if d < n_tp - 1:
                total_ref[:, cols] = part
            else:
                out_ref[:, cols] = part.astype(out_ref.dtype)

    for g in gcopies:
        g.wait_send()
    for line in first + last:
        for c in line:
            c.wait_send()
    for m in range(PIECES):
        for d in (0, 1):

            @pl.when(has_target(d))
            def _():
                for c in range(groups):
                    chain_copy(m, d, c).wait_send()

    for c in attc:
        c.wait_send()


def body(
    n_req,
    n_tp,
    q_proj,
    kv_proj,
    q_bias,
    kv_bias,
    prefix_kv,
    lengths,
    group_of,
    owner,
    positions,
    residual,
    out_weight,
):
    cap, feats = q_proj.shape[1:]
    total = prefix_kv.shape[1] * 2
    rows = total // (QUAD * PIECES)
    groups = owner.shape[0]
    width = residual.shape[2]
    smem = pl.BlockSpec(memory_space=pltpu.SMEM)
    anym = pl.BlockSpec(memory_space=pl.ANY)
    dma = pltpu.SemaphoreType.DMA

    out = pl.pallas_call(
        functools.partial(kernel, n_req, n_tp, groups),
        out_shape=jax.ShapeDtypeStruct((cap, width), BF16),
        in_specs=[smem] * 4 + [anym] * 7,
        out_specs=pl.BlockSpec(memory_space=pltpu.VMEM),
        scratch_shapes=[
            pltpu.VMEM((cap, feats), BF16),
            pltpu.VMEM((2 * cap, HD), BF16),
            pltpu.VMEM((feats,), BF16),
            pltpu.VMEM((2, HD), BF16),
            pltpu.VMEM((cap, width), BF16),
            pltpu.VMEM(out_weight.shape, BF16),
            pltpu.VMEM((feats, HD), BF16),
            pltpu.VMEM((max(2 * cap, 2 * QUAD * rows), HD), F32),
            pltpu.VMEM((feats, 1), F32),
            pltpu.VMEM((feats, 1), F32),
            pltpu.VMEM((feats, HD), F32),
            pltpu.VMEM((8, 128), jnp.int32),
            pltpu.VMEM((QUAD - 1, 8, 128), jnp.int32),
            pltpu.SMEM((QUAD - 1, 8, 128), jnp.int32),
            pltpu.VMEM((n_tp, cap, feats), BF16),
            pltpu.VMEM((cap, width), F32),
            [pltpu.VMEM((QUAD, rows, HD), BF16)] * PIECES,
            [pltpu.VMEM((2, groups, rows, HD), BF16)] * PIECES,
            [pltpu.VMEM((2, groups, rows, HD), BF16)] * PIECES,
            [pltpu.VMEM((QUAD - 1, rows, HD), BF16)] * PIECES,
            [pltpu.VMEM((QUAD, rows, HD), BF16)] * PIECES,
            dma((7 + PIECES,)),
            dma((PIECES, QUAD - 1)),
            dma((PIECES, QUAD - 1)),
            dma((PIECES, 2 * groups)),
            dma((PIECES, 2 * groups)),
            dma((PIECES, QUAD - 1)),
            dma((PIECES, QUAD - 1)),
            dma((QUAD - 1,)),
            dma((QUAD - 1,)),
            dma((max(n_tp - 1, 1),)),
            dma((max(n_tp - 1, 1),)),
        ],
        compiler_params=pltpu.CompilerParams(
            collective_id=0, has_side_effects=True, vmem_limit_bytes=60 * 1024 * 1024
        ),
        cost_estimate=pl.CostEstimate(
            flops=2 * cap * out_weight.shape[0] * width + 4 * cap * feats * (total // 2 + cap),
            bytes_accessed=2 * (out_weight.size + 2 * cap * width + total * HD),
            transcendentals=cap * feats // HD * (total // 2 + cap),
        ),
    )(
        lengths,
        group_of,
        owner,
        positions,
        q_proj[0],
        kv_proj[0].reshape(2 * cap, HD),
        q_bias,
        kv_bias,
        prefix_kv[0].reshape(total, HD),
        residual[0],
        out_weight,
    )
    return out[None]


def solution(mesh):
    in_specs = (
        P("req", None, "tp"),
        P("req", None, None, "tp"),
        P("tp"),
        P(None, "tp"),
        P("req", None, None, "tp"),
        P("req"),
        P("req"),
        P(),
        P("req", None),
        P("req", None, "tp"),
        P(None, "tp"),
    )
    out_specs = P("req", None, "tp")
    run = functools.partial(body, mesh.shape["req"], mesh.shape["tp"])
    return jax.shard_map(run, mesh=mesh, in_specs=in_specs, out_specs=out_specs, check_vma=False)
```
